32 devices in a mesh: rad: 8 (over z, x), azi: 2 (over y), ax: 2 (over core).
Axes of the slice: x: 2, y: 2, z: 4, core: 2. Of those that a mesh axis runs over, the one named last changes fastest.
Arguments:
- density: float32 [512, 16, 1024], P('rad', 'ax', 'azi'), may hold values from 0.5 to 2
- momentum: float32 [3, 512, 16, 1024], P(None, 'rad', 'ax', 'azi'), may hold values from -3 to 3
- energy: float32 [512, 16, 1024], P('rad', 'ax', 'azi'), may hold values from 2 to 4
- register: float32 [5, 512, 16, 1024], P(None, 'rad', 'ax', 'azi'), may hold values from -4 to 4
Outputs:
- register_new: float32 [5, 512, 16, 1024], P(None, 'rad', 'ax', 'azi')
- state_new: float32 [5, 512, 16, 1024], P(None, 'rad', 'ax', 'azi')
The draws below stay inside these ranges and needn't reach their ends.
All inputs are finite; a program needn't handle non-finite values.
Results may differ from the reference program's by a relative error of at most 0.00012.
Values sent between devices are 32-bit elements; how exact they have to be, the bound alone decides.
A program may use at most 128 MiB of HBM per device.

```python
import jax
import jax.numpy as jnp
from jax import lax

NTH = 1024
FIELDS = 5
NR = 512
NZ = 16


def block_scale(rng, shape, split, least, top_value):
    gain, own = 1.0, jax.random.fold_in(rng, 6)
    for position, shards_of in split:
        draws = jnp.exp(jax.random.uniform(jax.random.fold_in(own, position), (shards_of,), jnp.float32, least / len(split), top_value / len(split)))
        gain = gain * jnp.repeat(draws, shape[position] // shards_of).reshape([-1 if axis == position else 1 for axis in range(len(shape))])
    return gain


def scatter_about(stream_key, extent, deviation, limit, shards=(), kind=jnp.bfloat16):
    entries = deviation * jax.random.normal(stream_key, extent, jnp.float32)
    if shards:
        entries = entries * block_scale(stream_key, extent, shards, -0.22, 0.18)
    return jnp.clip(entries, -limit, limit).astype(kind)


def setup_inputs(seed: int = 0) -> dict:
    key_of = jax.random.split(jax.random.key(seed), 5)
    return {
        "density": jnp.clip(0.5 + 1.5 * jax.random.uniform(key_of[0], (NR, NZ, NTH), jnp.float32) ** block_scale(key_of[0], (NR, NZ, NTH), ((0, 8), (1, 2), (2, 2)), -0.2, 0.2), 0.5, 2.0),
        "momentum": scatter_about(key_of[1], (3, NR, NZ, NTH), 0.5, 3.0, ((1, 8), (2, 2), (3, 2)), jnp.float32),
        "energy": jnp.clip(2.0 + 2.0 * jax.random.uniform(key_of[2], (NR, NZ, NTH), jnp.float32) ** block_scale(key_of[2], (NR, NZ, NTH), ((0, 8), (1, 2), (2, 2)), -0.2, 0.2), 2.0, 4.0),
        "register": scatter_about(key_of[3], (FIELDS, NR, NZ, NTH), 0.5, 4.0, ((1, 8), (2, 2), (3, 2)), jnp.float32),
    }


HEAT_RATIO = 1.4
COURANT = 0.5
SECTION_DECAY = -5.0 / 9.0
SECTION_GAIN = 15.0 / 16.0
CUTOFF_BASE = 4.0
STENCIL = (0.8, -0.2, 4.0 / 105.0, -1.0 / 280.0)


def component(field_id, momentum, velocity, pressure, energy, direction):
    if field_id == 0:
        return momentum[direction]
    if field_id == 4:
        return (energy + pressure) * velocity[direction]
    flux_value = momentum[field_id - 1] * velocity[direction]
    if field_id - 1 == direction:
        flux_value = flux_value + pressure
    return flux_value


def central(padded, length, axis_id, spacing):
    summed = 0.0
    for offset, weight in enumerate(STENCIL, start=1):
        upper_rows = lax.slice_in_dim(padded, 4 + offset, 4 + offset + length, axis=axis_id)
        lower_rows = lax.slice_in_dim(padded, 4 - offset, 4 - offset + length, axis=axis_id)
        summed = summed + weight * (upper_rows - lower_rows)
    return summed / spacing


def reference(density, momentum, energy, register):
    radial_total, axial_total, circle_half = density.shape
    spacing = 2.0 / radial_total
    radius_col = (-1.0 + (jnp.arange(radial_total, dtype=jnp.float32) + 0.5) * spacing)[:, None, None]
    azimuths = jnp.pi * jnp.arange(circle_half, dtype=jnp.float32) / circle_half
    cosine = jnp.cos(azimuths)
    sine_col = jnp.sin(azimuths)
    velocity = momentum / density
    pressure = (HEAT_RATIO - 1.0) * (energy - 0.5 * jnp.sum(momentum * velocity, axis=0))
    halfway = radial_total // 2
    positive = radius_col[halfway:]
    mode_ids = jnp.arange(circle_half + 1, dtype=jnp.float32)
    cutoff = CUTOFF_BASE + circle_half * positive
    multiplier = jnp.where(mode_ids < circle_half, mode_ids, 0.0) / (1.0 + (mode_ids / cutoff) ** 8)
    signs = jnp.sign(radius_col)
    conserved = [density, momentum[0], momentum[1], momentum[2], energy]
    registers = []
    states = []
    for field_id in range(5):
        flux_x = component(field_id, momentum, velocity, pressure, energy, 0)
        flux_y = component(field_id, momentum, velocity, pressure, energy, 1)
        flux_z = component(field_id, momentum, velocity, pressure, energy, 2)
        radial_flux = radius_col * (cosine * flux_x + sine_col * flux_y)
        radial_term = central(jnp.pad(radial_flux, ((4, 4), (0, 0), (0, 0))), radial_total, 0, spacing) / radius_col
        azimuth_flux = signs * (cosine * flux_y - sine_col * flux_x)
        circle = jnp.concatenate([azimuth_flux[halfway:], azimuth_flux[:halfway][::-1]], axis=-1)
        spectrum = jnp.fft.rfft(circle, axis=-1)
        derived = jnp.fft.irfft(1j * multiplier * spectrum, n=2 * circle_half, axis=-1) / positive
        azimuthal_term = jnp.concatenate([derived[:, :, circle_half:][::-1], derived[:, :, :circle_half]], axis=0)
        axial_term = central(jnp.pad(flux_z, ((0, 0), (4, 4), (0, 0))), axial_total, 1, spacing)
        change = -(radial_term + azimuthal_term + axial_term)
        updated = SECTION_DECAY * register[field_id] + COURANT * spacing * change
        registers.append(updated)
        states.append(conserved[field_id] + SECTION_GAIN * updated)
    return jnp.stack(registers), jnp.stack(states)
```

```python
import numpy as np
import jax
import jax.numpy as jnp
from jax import lax
from jax.sharding import PartitionSpec as P

HEAT_RATIO = 1.4
COURANT = 0.5
SECTION_DECAY = -5.0 / 9.0
SECTION_GAIN = 15.0 / 16.0
CUTOFF_BASE = 4.0
STENCIL = (0.8, -0.2, 4.0 / 105.0, -1.0 / 280.0)
CUTS = 1
DEPTH = 2


def trig_tables(half):
    points = np.arange(half)[:, None]
    tables = []
    for modes in (np.arange(0, half, 2), np.arange(1, half, 2)):
        phases = (points * modes[None, :] % (2 * half)) * (np.pi / half)
        tables.append(np.concatenate([np.cos(phases), np.sin(phases)], axis=1).astype(np.float32))
    return tables


def padded_2(block, axis, dim, width):
    count = lax.axis_size(axis)
    forward = [(i, i + 1) for i in range(count - 1)]
    backward = [(target, source) for source, target in forward]
    low = lax.ppermute(lax.slice_in_dim(block, block.shape[dim] - width, None, axis=dim), axis, forward)
    high = lax.ppermute(lax.slice_in_dim(block, 0, width, axis=dim), axis, backward)
    return low, high


def central(padded, length, axis_id, spacing):
    summed = 0.0
    for offset, weight in enumerate(STENCIL, start=1):
        upper_rows = lax.slice_in_dim(padded, 4 + offset, 4 + offset + length, axis=axis_id)
        lower_rows = lax.slice_in_dim(padded, 4 - offset, 4 - offset + length, axis=axis_id)
        summed = summed + weight * (upper_rows - lower_rows)
    return summed / spacing


def component(field_id, momentum, velocity, pressure, energy, direction):
    if field_id == 0:
        return momentum[direction]
    if field_id == 4:
        return (energy + pressure) * velocity[direction]
    flux_value = momentum[field_id - 1] * velocity[direction]
    if field_id - 1 == direction:
        flux_value = flux_value + pressure
    return flux_value


def per_device(density, momentum, energy, register):
    slabs = lax.axis_size("rad")
    blocks = lax.axis_size("azi")
    rad_index = lax.axis_index("rad")
    azi_index = lax.axis_index("azi")
    row_count, plane_count, angles = density.shape
    radial_total = row_count * slabs
    half = angles * blocks
    spacing = 2.0 / radial_total
    row_ids = rad_index * row_count + jnp.arange(row_count, dtype=jnp.int32)
    radius_col = (-1.0 + (row_ids.astype(jnp.float32) + 0.5) * spacing)[:, None, None]
    column_ids = azi_index * angles + jnp.arange(angles, dtype=jnp.int32)
    azimuths = jnp.pi * column_ids.astype(jnp.float32) / half
    cosine = jnp.cos(azimuths)
    sine_col = jnp.sin(azimuths)
    upper = rad_index >= slabs // 2
    group_rows = row_count // blocks
    cuts = CUTS if group_rows % CUTS == 0 else 1
    piece = group_rows // cuts

    velocity = momentum / density
    pressure = (HEAT_RATIO - 1.0) * (energy - 0.5 * jnp.sum(momentum * velocity, axis=0))
    conserved = [density, momentum[0], momentum[1], momentum[2], energy]

    def flux(field_id, direction):
        return component(field_id, momentum, velocity, pressure, energy, direction)

    sign = jnp.where(upper, 1.0, -1.0).astype(jnp.float32)
    azimuth_flux = [
        (sign * cosine) * flux(f, 1) - (sign * sine_col) * flux(f, 0) for f in range(5)
    ]

    even_table, odd_table = trig_tables(half)
    mode_even = jnp.arange(0, half, 2, dtype=jnp.int32).astype(jnp.float32)
    mode_odd = jnp.arange(1, half, 2, dtype=jnp.int32).astype(jnp.float32)

    def group_of(member):
        return jnp.where(upper, member, blocks - 1 - member)

    mirror = [
        (r * blocks + a, (slabs - 1 - r) * blocks + a) for r in range(slabs) for a in range(blocks)
    ]

    def start_of(member, part):
        inner = jnp.where(upper, part, cuts - 1 - part)
        return group_of(member) * group_rows + inner * piece

    def gather_azi(values, part):
        whole = jnp.zeros((piece, plane_count, half), jnp.float32)
        own = lax.dynamic_slice_in_dim(values, start_of(azi_index, part), piece, 0)
        whole = lax.dynamic_update_slice_in_dim(whole, own, azi_index * angles, 2)
        for shift in range(1, blocks):
            target = (azi_index + shift) % blocks
            source = (azi_index + blocks - shift) % blocks
            sent = lax.dynamic_slice_in_dim(values, start_of(target, part), piece, 0)
            got = lax.ppermute(sent, "azi", [(a, (a + shift) % blocks) for a in range(blocks)])
            whole = lax.dynamic_update_slice_in_dim(whole, got, source * angles, 2)
        return whole

    def derive(own, other, part):
        rows = rad_index * row_count + start_of(azi_index, part) + jnp.arange(piece, dtype=jnp.int32)
        distance = jnp.abs(-1.0 + (rows.astype(jnp.float32) + 0.5) * spacing)[:, None, None]
        cutoff = CUTOFF_BASE + half * distance
        result = 0.0
        for values, table, modes in (
            (own + other, even_table, mode_even),
            (own - other, odd_table, mode_odd),
        ):
            filtered = modes / half / (1.0 + (modes / cutoff) ** 8) / distance
            sums = lax.dot_general(
                values.reshape(piece * plane_count, half), table, (((1,), (0,)), ((), ())),
                precision=lax.Precision.HIGH, preferred_element_type=jnp.float32,
            ).reshape(piece, plane_count, half)
            turned = jnp.concatenate(
                [filtered * sums[..., half // 2 :], -filtered * sums[..., : half // 2]], axis=-1
            )
            result = result + lax.dot_general(
                turned.reshape(piece * plane_count, half), table, (((1,), (1,)), ((), ())),
                precision=lax.Precision.HIGH, preferred_element_type=jnp.float32,
            )
        return result.reshape(piece, plane_count, half)

    def scatter_azi(total, values, part):
        own = lax.dynamic_slice_in_dim(values, azi_index * angles, angles, 2)
        total = lax.dynamic_update_slice_in_dim(total, own, start_of(azi_index, part), 0)
        for shift in range(1, blocks):
            target = (azi_index + shift) % blocks
            source = (azi_index + blocks - shift) % blocks
            sent = lax.dynamic_slice_in_dim(values, target * angles, angles, 2)
            got = lax.ppermute(sent, "azi", [(a, (a + shift) % blocks) for a in range(blocks)])
            total = lax.dynamic_update_slice_in_dim(total, got, start_of(source, part), 0)
        return total

    steps = [(f, part) for f in range(5) for part in range(cuts)]
    azimuthal = [jnp.zeros((row_count, plane_count, angles), jnp.float32) for _ in range(5)]
    arrived = []
    for index, (f, part) in enumerate(steps):
        own = gather_azi(azimuth_flux[f], part)
        if index >= DEPTH:
            own, arrived[index - DEPTH] = lax.optimization_barrier((own, arrived[index - DEPTH]))
        other = lax.ppermute(own, ("rad", "azi"), mirror)
        arrived.append((own, other))
    for index, (f, part) in enumerate(steps):
        own, other = arrived[index]
        derived = derive(own, jnp.flip(other, 0), part)
        azimuthal[f] = scatter_azi(azimuthal[f], derived, part)

    flux_x, flux_y, flux_z = (jnp.stack([flux(f, c) for f in range(5)]) for c in range(3))
    radial_flux = radius_col * (cosine * flux_x + sine_col * flux_y)
    low, high = padded_2(radial_flux, "rad", 1, 4)
    radial_padded = jnp.concatenate([low, radial_flux, high], axis=1)
    low, high = padded_2(flux_z, "ax", 2, 4)
    axial_padded = jnp.concatenate([low, flux_z, high], axis=2)
    radial_term = central(radial_padded, row_count, 1, spacing) / radius_col
    axial_term = central(axial_padded, plane_count, 2, spacing)
    base = SECTION_DECAY * register - COURANT * spacing * (radial_term + axial_term)
    base = lax.optimization_barrier(base)
    register_new = jnp.stack([base[f] - COURANT * spacing * azimuthal[f] for f in range(5)])
    state_new = jnp.stack(conserved) + SECTION_GAIN * register_new
    return (register_new, state_new)


def solution(mesh):
    placed = (
        P("rad", "ax", "azi"),
        P(None, "rad", "ax", "azi"),
        P("rad", "ax", "azi"),
        P(None, "rad", "ax", "azi"),
    )
    return jax.shard_map(
        per_device,
        mesh=mesh,
        in_specs=placed,
        out_specs=(P(None, "rad", "ax", "azi"), P(None, "rad", "ax", "azi")),
        check_vma=False,
    )
```

```python
import functools

import numpy as np
import jax
import jax.numpy as jnp
from jax import lax
from jax.experimental import pallas as pl
from jax.experimental.pallas import tpu as pltpu
from jax.sharding import PartitionSpec as P

HEAT_RATIO = 1.4
COURANT = 0.5
SECTION_DECAY = -5.0 / 9.0
SECTION_GAIN = 15.0 / 16.0
CUTOFF_BASE = 4.0
STENCIL = (0.8, -0.2, 4.0 / 105.0, -1.0 / 280.0)
FIELDS = 5
DEPTH = 2
MESH = pl.DeviceIdType.MESH


def trig_tables(half):
    points = np.arange(half)[:, None]
    tables = []
    for modes in (np.arange(0, half, 2), np.arange(1, half, 2)):
        phases = (points * modes[None, :] % (2 * half)) * (np.pi / half)
        tables.append(np.concatenate([np.cos(phases), np.sin(phases)], axis=1).astype(np.float32))
    table = np.stack(tables)
    high = table.astype(jnp.bfloat16)
    low = (table - high.astype(np.float32)).astype(jnp.bfloat16)
    return high, low


def split(values):
    high = values.astype(jnp.bfloat16)
    return high, (values - high.astype(jnp.float32)).astype(jnp.bfloat16)


def product(left_high, left_low, right_high, right_low, dims):
    dot = functools.partial(
        lax.dot_general, dimension_numbers=(dims, ((), ())), preferred_element_type=jnp.float32
    )
    return dot(left_high, right_high) + (dot(left_low, right_high) + dot(left_high, right_low))


def kernel(
    slabs, blocks, spacing,
    density, momentum, energy, trig, filt, table_high, table_low,
    out,
    g, rf, fz, fzr, ownx, other, az, xh, xl, yh, yl,
    zs, zr, ys, yr, rs, rr, hs, hr,
):
    rad, azi, ax = lax.axis_index("rad"), lax.axis_index("azi"), lax.axis_index("ax")
    rows, planes, angles = density.shape
    half = angles * blocks
    group = rows // blocks
    lines = group * planes
    mirror = slabs - 1 - rad
    upper = rad >= slabs // 2
    has_low, has_high = rad > 0, rad < slabs - 1

    def group_of(member):
        return jnp.where(upper, member, blocks - 1 - member) * group

    def peer(shift):
        return lax.rem(azi + shift, blocks)

    mine = group_of(azi)

    barrier = pltpu.get_barrier_semaphore()

    def greet(target):
        pl.semaphore_signal(barrier, inc=1, device_id=target, device_id_type=MESH)

    for shift in range(blocks):
        greet((mirror, peer(shift), ax))
        if shift:
            greet((rad, peer(shift), ax))
    greet((rad, azi, 1 - ax))

    @pl.when(has_low)
    def _():
        greet((rad - 1, azi, ax))

    @pl.when(has_high)
    def _():
        greet((rad + 1, azi, ax))

    def flux_row(l, _):
        rho, en = density[l], energy[l]
        mom = [momentum[c, l] for c in range(3)]
        inverse = 1.0 / rho
        vel = [m * inverse for m in mom]
        kinetic = mom[0] * vel[0] + mom[1] * vel[1] + mom[2] * vel[2]
        pressure = (HEAT_RATIO - 1.0) * (en - 0.5 * kinetic)
        radius = -1.0 + ((rad * rows + l).astype(jnp.float32) + 0.5) * spacing
        cosine, sine = trig[0], trig[1]
        scos, ssin = trig[2], trig[3]
        for f in range(FIELDS):
            parts = []
            for c in range(3):
                if f == 0:
                    value = mom[c]
                elif f == 4:
                    value = (en + pressure) * vel[c]
                else:
                    value = mom[f - 1] * vel[c]
                    if f - 1 == c:
                        value = value + pressure
                parts.append(value)
            g[f, l] = scos * parts[1] - ssin * parts[0]
            rf[f, l + 4] = radius * (cosine * parts[0] + sine * parts[1])
            fz[f, l] = parts[2]
        return 0

    lax.fori_loop(0, rows, flux_row, 0)

    pl.semaphore_wait(
        barrier, 2 * blocks + has_low.astype(jnp.int32) + has_high.astype(jnp.int32)
    )

    def remote(source, target, send, recv, device):
        return pltpu.make_async_remote_copy(
            src_ref=source, dst_ref=target, send_sem=send, recv_sem=recv,
            device_id=device, device_id_type=MESH,
        )

    to_high = remote(
        rf.at[:, pl.ds(rows, 4)], rf.at[:, pl.ds(0, 4)], hs.at[0], hr.at[0],
        (jnp.minimum(rad + 1, slabs - 1), azi, ax),
    )
    to_low = remote(
        rf.at[:, pl.ds(4, 4)], rf.at[:, pl.ds(rows + 4, 4)], hs.at[1], hr.at[1],
        (jnp.maximum(rad - 1, 0), azi, ax),
    )
    across = remote(fz, fzr, hs.at[2], hr.at[2], (rad, azi, 1 - ax))

    def z_copy(f, member, slot):
        return remote(
            g.at[f, pl.ds(group_of(member), group)], other.at[f, slot],
            zs.at[f, member], zr.at[f, slot], (mirror, member, ax),
        )

    def y_copy(f, member, slot):
        return remote(
            g.at[f, pl.ds(group_of(member), group)], ownx.at[f, slot],
            ys.at[f, member], yr.at[f, slot], (rad, member, ax),
        )

    def r_copy(f, member, source):
        return remote(
            g.at[f, pl.ds(member * group, group)], az.at[f, pl.ds(group_of(source), group)],
            rs.at[f, member], rr.at[f, source], (rad, member, ax),
        )

    def launch(f):
        for shift in range(blocks):
            z_copy(f, peer(shift), azi).start()
        for shift in range(1, blocks):
            y_copy(f, peer(shift), azi).start()

    @pl.when(has_high)
    def _():
        to_high.start()

    @pl.when(has_low)
    def _():
        to_low.start()

    for f in range(DEPTH):
        launch(f)
    across.start()

    @pl.when(jnp.logical_not(has_low))
    def _():
        rf[:, pl.ds(0, 4)] = jnp.zeros((FIELDS, 4, planes, angles), jnp.float32)

    @pl.when(jnp.logical_not(has_high))
    def _():
        rf[:, pl.ds(rows + 4, 4)] = jnp.zeros((FIELDS, 4, planes, angles), jnp.float32)

    @pl.when(has_low)
    def _():
        to_high.wait_recv()
        to_low.wait_send()

    @pl.when(has_high)
    def _():
        to_low.wait_recv()
        to_high.wait_send()

    across.wait()
    is_first = jnp.where(ax == 0, 1.0, 0.0).astype(jnp.float32)
    plane_ids = lax.broadcasted_iota(jnp.int32, (planes, angles), 0)

    def local_row(l, _):
        radius = -1.0 + ((rad * rows + l).astype(jnp.float32) + 0.5) * spacing
        scale = 1.0 / (jnp.full((planes, angles), spacing, jnp.float32) * radius)
        for f in range(FIELDS):
            radial = 0.0
            axial = 0.0
            own, far = fz[f, l], fzr[f, l]
            high, low = far * is_first, far * (1.0 - is_first)
            for m, weight in enumerate(STENCIL, start=1):
                radial = radial + weight * (rf[f, l + 4 + m] - rf[f, l + 4 - m])
                ahead = pltpu.roll(jnp.where(plane_ids < m, high, own), planes - m, 0)
                behind = pltpu.roll(jnp.where(plane_ids >= planes - m, low, own), m, 0)
                axial = axial + weight * (ahead - behind)
            out[f, l] = radial * scale + axial * (1.0 / spacing)
        return 0

    lax.fori_loop(0, rows, local_row, 0)

    tile = min(256, half)
    point_tile = min(256, angles)
    quarters = half // tile

    def add_in(f):
        for shift in range(1, blocks):
            source = peer(shift)
            r_copy(f, source, source).wait_recv()

        def add_row(l, _):
            out[f, l] = out[f, l] + az[f, l]
            return 0

        lax.fori_loop(0, rows, add_row, 0)

    def step(f, _):
        for shift in range(blocks):
            z_copy(f, peer(shift), peer(shift)).wait_recv()
        for shift in range(1, blocks):
            y_copy(f, peer(shift), peer(shift)).wait_recv()

        @pl.when(f + DEPTH < FIELDS)
        def _():
            launch(f + DEPTH)

        for shift in range(blocks):
            z_copy(f, peer(shift), azi).wait_send()
        for shift in range(1, blocks):
            y_copy(f, peer(shift), azi).wait_send()

        def copy_own(i, _):
            ownx[f, azi, i] = g[f, mine + i]
            return 0

        lax.fori_loop(0, group, copy_own, 0)

        def mix(i, _):
            j, k = i // (group // 2), lax.rem(i, group // 2)
            near = jnp.concatenate([ownx[f, j, 2 * k], ownx[f, j, 2 * k + 1]], axis=0)
            back = group - 1 - 2 * k
            far = jnp.concatenate([other[f, j, back], other[f, j, back - 1]], axis=0)
            place = pl.ds(pl.multiple_of(k * 2 * planes, 2 * planes), 2 * planes)
            for par, value in enumerate((near + far, near - far)):
                top, rest = split(value)
                xh[par, j, place] = top
                xl[par, j, place] = rest
            return 0

        lax.fori_loop(0, blocks * group // 2, mix, 0)

        def forward(i, _):
            par, t = i // quarters, lax.rem(i, quarters)
            columns = pl.ds(pl.multiple_of(t * tile, tile), tile)
            total = jnp.zeros((lines, tile), jnp.float32)
            for j in range(blocks):
                total = total + product(
                    xh[par, j], xl[par, j],
                    table_high[par, j, :, columns], table_low[par, j, :, columns], ((1,), (0,)),
                )
            scaled = total * filt[par, :, columns]
            moved = lax.rem(t + quarters // 2, quarters)
            target = pl.ds(pl.multiple_of(moved * tile, tile), tile)
            top, rest = split(scaled)
            yh[par, :, target] = top
            yl[par, :, target] = rest
            return 0

        lax.fori_loop(0, 2 * quarters, forward, 0)

        def inverse(i, _):
            per = angles // point_tile
            j, p = i // per, lax.rem(i, per)
            points = pl.ds(pl.multiple_of(p * point_tile, point_tile), point_tile)
            total = 0.0
            for par in range(2):
                total = total + product(
                    yh[par], yl[par], table_high[par, j, points, :], table_low[par, j, points, :],
                    ((1,), (1,)),
                )
            g[f, pl.ds(j * group, group), :, points] = total.reshape(group, planes, point_tile)
            return 0

        lax.fori_loop(0, blocks * (angles // point_tile), inverse, 0)

        for shift in range(1, blocks):
            r_copy(f, peer(shift), azi).start()

        def keep_own(i, _):
            az[f, mine + i] = g[f, azi * group + i]
            return 0

        lax.fori_loop(0, group, keep_own, 0)

        @pl.when(f >= 1)
        def _():
            add_in(f - 1)

        return 0

    lax.fori_loop(0, FIELDS, step, 0)
    add_in(FIELDS - 1)
    for f in range(FIELDS):
        for shift in range(1, blocks):
            r_copy(f, peer(shift), azi).wait_send()


def per_device(density, momentum, energy, register):
    slabs = lax.axis_size("rad")
    blocks = lax.axis_size("azi")
    rad_index = lax.axis_index("rad")
    azi_index = lax.axis_index("azi")
    rows, planes, angles = density.shape
    half = angles * blocks
    spacing = 2.0 / (rows * slabs)
    group = rows // blocks
    lines = group * planes
    upper = rad_index >= slabs // 2

    azimuths = jnp.pi * (azi_index * angles + jnp.arange(angles)).astype(jnp.float32) / half
    cosine, sine = jnp.cos(azimuths), jnp.sin(azimuths)
    sign = jnp.where(upper, 1.0, -1.0).astype(jnp.float32)
    trig = jnp.broadcast_to(
        jnp.stack([cosine, sine, sign * cosine, sign * sine])[:, None, :], (4, planes, angles)
    )
    mine = jnp.where(upper, azi_index, blocks - 1 - azi_index) * group
    row_ids = rad_index * rows + mine + jnp.arange(group)
    distance = jnp.abs(-1.0 + (row_ids.astype(jnp.float32) + 0.5) * spacing)[None, :, None]
    modes = jnp.stack([jnp.arange(0, half, 2), jnp.arange(1, half, 2)]).astype(jnp.float32)[:, None]
    weight = modes / half / (1.0 + (modes / (CUTOFF_BASE + half * distance)) ** 8) / distance
    weight = jnp.concatenate([-weight, weight], axis=-1)
    filt = jnp.broadcast_to(weight[:, :, None, :], (2, group, planes, half)).reshape(2, lines, half)
    high, low = trig_tables(half)
    high = high.reshape(2, blocks, angles, half)
    low = low.reshape(2, blocks, angles, half)

    f32, bf16 = jnp.float32, jnp.bfloat16
    vmem, dma = pltpu.VMEM, pltpu.SemaphoreType.DMA
    block = (FIELDS, rows, planes, angles)
    pieces = (FIELDS, blocks, group, planes, angles)
    term = pl.pallas_call(
        functools.partial(kernel, slabs, blocks, spacing),
        out_shape=jax.ShapeDtypeStruct(block, f32),
        in_specs=[pl.BlockSpec(memory_space=pltpu.VMEM)] * 7,
        out_specs=pl.BlockSpec(memory_space=pltpu.VMEM),
        scratch_shapes=[
            vmem(block, f32),
            vmem((FIELDS, rows + 8, planes, angles), f32),
            vmem(block, f32),
            vmem(block, f32),
            vmem(pieces, f32),
            vmem(pieces, f32),
            vmem(block, f32),
            vmem((2, blocks, lines, angles), bf16),
            vmem((2, blocks, lines, angles), bf16),
            vmem((2, lines, half), bf16),
            vmem((2, lines, half), bf16),
        ] + [dma((FIELDS, blocks))] * 6 + [dma((3,))] * 2,
        compiler_params=pltpu.CompilerParams(
            collective_id=0, has_side_effects=True, vmem_limit_bytes=63 * 2**20
        ),
    )(density, momentum, energy, trig, filt, jnp.asarray(high), jnp.asarray(low))
    conserved = jnp.concatenate([density[None], momentum, energy[None]], axis=0)
    register_new = SECTION_DECAY * register - COURANT * spacing * term
    state_new = conserved + SECTION_GAIN * register_new
    return (register_new, state_new)


def solution(mesh):
    placed = (
        P("rad", "ax", "azi"),
        P(None, "rad", "ax", "azi"),
        P("rad", "ax", "azi"),
        P(None, "rad", "ax", "azi"),
    )
    return jax.shard_map(
        per_device,
        mesh=mesh,
        in_specs=placed,
        out_specs=(P(None, "rad", "ax", "azi"), P(None, "rad", "ax", "azi")),
        check_vma=False,
    )
```

```python
import functools

import numpy as np
import jax
import jax.numpy as jnp
from jax import lax
from jax.experimental import pallas as pl
from jax.experimental.pallas import tpu as pltpu
from jax.sharding import PartitionSpec as P

HEAT_RATIO = 1.4
COURANT = 0.5
SECTION_DECAY = -5.0 / 9.0
SECTION_GAIN = 15.0 / 16.0
CUTOFF_BASE = 4.0
STENCIL = (0.8, -0.2, 4.0 / 105.0, -1.0 / 280.0)
FIELDS = 5
EARLY = 2
MESH = pl.DeviceIdType.MESH


def trig_tables(half):
    points = np.arange(half)[:, None]
    tables = []
    for modes in (np.arange(0, half, 2), np.arange(1, half, 2)):
        phases = (points * modes[None, :] % (2 * half)) * (np.pi / half)
        tables.append(np.concatenate([np.cos(phases), np.sin(phases)], axis=1).astype(np.float32))
    table = np.stack(tables)
    high = table.astype(jnp.bfloat16)
    low = (table - high.astype(np.float32)).astype(jnp.bfloat16)
    return high, low


def split(values):
    high = values.astype(jnp.bfloat16)
    return high, (values - high.astype(jnp.float32)).astype(jnp.bfloat16)


def product(left_high, left_low, right_high, right_low, dims):
    dot = functools.partial(
        lax.dot_general, dimension_numbers=(dims, ((), ())), preferred_element_type=jnp.float32
    )
    return dot(left_high, right_high) + (dot(left_low, right_high) + dot(left_high, right_low))


def kernel(
    slabs, blocks, spacing,
    density, momentum, energy, trig, filt, table_high, table_low,
    out,
    g, rf, fz, fzr, ownx, other, az, xh, xl, yh, yl,
    zs, zr, ys, yr, rs, rr, hs, hr,
):
    rad, azi, ax = lax.axis_index("rad"), lax.axis_index("azi"), lax.axis_index("ax")
    rows, planes, angles = density.shape
    half = angles * blocks
    group = rows // blocks
    lines = group * planes
    mirror = slabs - 1 - rad
    upper = rad >= slabs // 2
    has_low, has_high = rad > 0, rad < slabs - 1

    def group_of(member):
        return jnp.where(upper, member, blocks - 1 - member) * group

    def peer(shift):
        return lax.rem(azi + shift, blocks)

    mine = group_of(azi)

    barrier = pltpu.get_barrier_semaphore()

    def greet(target):
        pl.semaphore_signal(barrier, inc=1, device_id=target, device_id_type=MESH)

    for shift in range(blocks):
        greet((mirror, peer(shift), ax))
        if shift:
            greet((rad, peer(shift), ax))
    greet((rad, azi, 1 - ax))

    @pl.when(has_low)
    def _():
        greet((rad - 1, azi, ax))

    @pl.when(has_high)
    def _():
        greet((rad + 1, azi, ax))

    def flux_row(l, _):
        rho, en = density[l], energy[l]
        mom = [momentum[c, l] for c in range(3)]
        inverse = 1.0 / rho
        vel = [m * inverse for m in mom]
        kinetic = mom[0] * vel[0] + mom[1] * vel[1] + mom[2] * vel[2]
        pressure = (HEAT_RATIO - 1.0) * (en - 0.5 * kinetic)
        radius = -1.0 + ((rad * rows + l).astype(jnp.float32) + 0.5) * spacing
        cosine, sine = trig[0], trig[1]
        scos, ssin = trig[2], trig[3]
        for f in range(FIELDS):
            parts = []
            for c in range(3):
                if f == 0:
                    value = mom[c]
                elif f == 4:
                    value = (en + pressure) * vel[c]
                else:
                    value = mom[f - 1] * vel[c]
                    if f - 1 == c:
                        value = value + pressure
                parts.append(value)
            g[f, l] = scos * parts[1] - ssin * parts[0]
            rf[f, l + 4] = radius * (cosine * parts[0] + sine * parts[1])
            fz[f, l] = parts[2]
        return 0

    lax.fori_loop(0, rows, flux_row, 0)

    pl.semaphore_wait(
        barrier, 2 * blocks + has_low.astype(jnp.int32) + has_high.astype(jnp.int32)
    )

    def remote(source, target, send, recv, device):
        return pltpu.make_async_remote_copy(
            src_ref=source, dst_ref=target, send_sem=send, recv_sem=recv,
            device_id=device, device_id_type=MESH,
        )

    to_high = remote(
        rf.at[:, pl.ds(rows, 4)], rf.at[:, pl.ds(0, 4)], hs.at[0], hr.at[0],
        (jnp.minimum(rad + 1, slabs - 1), azi, ax),
    )
    to_low = remote(
        rf.at[:, pl.ds(4, 4)], rf.at[:, pl.ds(rows + 4, 4)], hs.at[1], hr.at[1],
        (jnp.maximum(rad - 1, 0), azi, ax),
    )
    across = remote(fz, fzr, hs.at[2], hr.at[2], (rad, azi, 1 - ax))

    def z_copy(f):
        return remote(
            g.at[f, pl.ds(mine, group)], other.at[f, azi],
            zs.at[f, azi], zr.at[f, azi], (mirror, azi, ax),
        )

    def forward_copy(f, member):
        return remote(
            ownx.at[f, member], other.at[f, member],
            zs.at[f, member], zr.at[f, member], (mirror, azi, ax),
        )

    def y_copy(f, member, slot):
        return remote(
            g.at[f, pl.ds(group_of(member), group)], ownx.at[f, slot],
            ys.at[f, member], yr.at[f, slot], (rad, member, ax),
        )

    def r_copy(f, member, source):
        return remote(
            g.at[f, pl.ds(member * group, group)], az.at[f, pl.ds(group_of(source), group)],
            rs.at[f, member], rr.at[f, source], (rad, member, ax),
        )

    def launch(f):
        for shift in range(1, blocks):
            y_copy(f, peer(shift), azi).start()
        z_copy(f).start()

    def pass_on(f):
        for shift in range(1, blocks):
            y_copy(f, peer(shift), peer(shift)).wait_recv()
            forward_copy(f, peer(shift)).start()

    @pl.when(has_high)
    def _():
        to_high.start()

    @pl.when(has_low)
    def _():
        to_low.start()

    for f in range(FIELDS):
        launch(f)
    across.start()
    for f in range(EARLY):
        pass_on(f)

    @pl.when(jnp.logical_not(has_low))
    def _():
        rf[:, pl.ds(0, 4)] = jnp.zeros((FIELDS, 4, planes, angles), jnp.float32)

    @pl.when(jnp.logical_not(has_high))
    def _():
        rf[:, pl.ds(rows + 4, 4)] = jnp.zeros((FIELDS, 4, planes, angles), jnp.float32)

    @pl.when(has_low)
    def _():
        to_high.wait_recv()
        to_low.wait_send()

    @pl.when(has_high)
    def _():
        to_low.wait_recv()
        to_high.wait_send()

    across.wait()
    is_first = jnp.where(ax == 0, 1.0, 0.0).astype(jnp.float32)
    plane_ids = lax.broadcasted_iota(jnp.int32, (planes, angles), 0)

    def local_row(l, _):
        radius = -1.0 + ((rad * rows + l).astype(jnp.float32) + 0.5) * spacing
        scale = 1.0 / (jnp.full((planes, angles), spacing, jnp.float32) * radius)
        for f in range(FIELDS):
            radial = 0.0
            axial = 0.0
            own, far = fz[f, l], fzr[f, l]
            high, low = far * is_first, far * (1.0 - is_first)
            for m, weight in enumerate(STENCIL, start=1):
                radial = radial + weight * (rf[f, l + 4 + m] - rf[f, l + 4 - m])
                ahead = pltpu.roll(jnp.where(plane_ids < m, high, own), planes - m, 0)
                behind = pltpu.roll(jnp.where(plane_ids >= planes - m, low, own), m, 0)
                axial = axial + weight * (ahead - behind)
            out[f, l] = radial * scale + axial * (1.0 / spacing)
        return 0

    lax.fori_loop(0, rows, local_row, 0)
    for f in range(EARLY, FIELDS):
        pass_on(f)

    tile = min(256, half)
    point_tile = min(256, angles)
    quarters = half // tile

    def add_in(f):
        for shift in range(1, blocks):
            source = peer(shift)
            r_copy(f, source, source).wait_recv()

        def add_row(l, _):
            out[f, l] = out[f, l] + az[f, l]
            return 0

        lax.fori_loop(0, rows, add_row, 0)

    def step(f, _):
        z_copy(f).wait()
        for shift in range(1, blocks):
            forward_copy(f, peer(shift)).wait()
            y_copy(f, peer(shift), azi).wait_send()

        def copy_own(i, _):
            ownx[f, azi, i] = g[f, mine + i]
            return 0

        lax.fori_loop(0, group, copy_own, 0)

        def mix(i, _):
            j, k = i // (group // 2), lax.rem(i, group // 2)
            near = jnp.concatenate([ownx[f, j, 2 * k], ownx[f, j, 2 * k + 1]], axis=0)
            back = group - 1 - 2 * k
            far = jnp.concatenate([other[f, j, back], other[f, j, back - 1]], axis=0)
            place = pl.ds(pl.multiple_of(k * 2 * planes, 2 * planes), 2 * planes)
            for par, value in enumerate((near + far, near - far)):
                top, rest = split(value)
                xh[par, j, place] = top
                xl[par, j, place] = rest
            return 0

        lax.fori_loop(0, blocks * group // 2, mix, 0)

        def forward(i, _):
            par, t = i // quarters, lax.rem(i, quarters)
            columns = pl.ds(pl.multiple_of(t * tile, tile), tile)
            total = jnp.zeros((lines, tile), jnp.float32)
            for j in range(blocks):
                total = total + product(
                    xh[par, j], xl[par, j],
                    table_high[par, j, :, columns], table_low[par, j, :, columns], ((1,), (0,)),
                )
            scaled = total * filt[par, :, columns]
            moved = lax.rem(t + quarters // 2, quarters)
            target = pl.ds(pl.multiple_of(moved * tile, tile), tile)
            top, rest = split(scaled)
            yh[par, :, target] = top
            yl[par, :, target] = rest
            return 0

        lax.fori_loop(0, 2 * quarters, forward, 0)

        per = angles // point_tile

        def inverse(i, _):
            j, p = lax.rem(azi + 1 + i // per, blocks), lax.rem(i, per)
            points = pl.ds(pl.multiple_of(p * point_tile, point_tile), point_tile)
            total = 0.0
            for par in range(2):
                total = total + product(
                    yh[par], yl[par], table_high[par, j, points, :], table_low[par, j, points, :],
                    ((1,), (1,)),
                )
            g[f, pl.ds(j * group, group), :, points] = total.reshape(group, planes, point_tile)
            return 0

        lax.fori_loop(0, (blocks - 1) * per, inverse, 0)
        for shift in range(1, blocks):
            r_copy(f, peer(shift), azi).start()
        lax.fori_loop((blocks - 1) * per, blocks * per, inverse, 0)

        def keep_own(i, _):
            az[f, mine + i] = g[f, azi * group + i]
            return 0

        lax.fori_loop(0, group, keep_own, 0)

        @pl.when(f >= 1)
        def _():
            add_in(f - 1)

        return 0

    lax.fori_loop(0, FIELDS, step, 0)
    add_in(FIELDS - 1)
    for f in range(FIELDS):
        for shift in range(1, blocks):
            r_copy(f, peer(shift), azi).wait_send()


def per_device(density, momentum, energy, register):
    slabs = lax.axis_size("rad")
    blocks = lax.axis_size("azi")
    rad_index = lax.axis_index("rad")
    azi_index = lax.axis_index("azi")
    rows, planes, angles = density.shape
    half = angles * blocks
    spacing = 2.0 / (rows * slabs)
    group = rows // blocks
    lines = group * planes
    upper = rad_index >= slabs // 2

    azimuths = jnp.pi * (azi_index * angles + jnp.arange(angles)).astype(jnp.float32) / half
    cosine, sine = jnp.cos(azimuths), jnp.sin(azimuths)
    sign = jnp.where(upper, 1.0, -1.0).astype(jnp.float32)
    trig = jnp.broadcast_to(
        jnp.stack([cosine, sine, sign * cosine, sign * sine])[:, None, :], (4, planes, angles)
    )
    mine = jnp.where(upper, azi_index, blocks - 1 - azi_index) * group
    row_ids = rad_index * rows + mine + jnp.arange(group)
    distance = jnp.abs(-1.0 + (row_ids.astype(jnp.float32) + 0.5) * spacing)[None, :, None]
    modes = jnp.stack([jnp.arange(0, half, 2), jnp.arange(1, half, 2)]).astype(jnp.float32)[:, None]
    weight = modes / half / (1.0 + (modes / (CUTOFF_BASE + half * distance)) ** 8) / distance
    weight = jnp.concatenate([-weight, weight], axis=-1)
    filt = jnp.broadcast_to(weight[:, :, None, :], (2, group, planes, half)).reshape(2, lines, half)
    high, low = trig_tables(half)
    high = high.reshape(2, blocks, angles, half)
    low = low.reshape(2, blocks, angles, half)

    f32, bf16 = jnp.float32, jnp.bfloat16
    vmem, dma = pltpu.VMEM, pltpu.SemaphoreType.DMA
    block = (FIELDS, rows, planes, angles)
    pieces = (FIELDS, blocks, group, planes, angles)
    term = pl.pallas_call(
        functools.partial(kernel, slabs, blocks, spacing),
        out_shape=jax.ShapeDtypeStruct(block, f32),
        in_specs=[pl.BlockSpec(memory_space=pltpu.VMEM)] * 7,
        out_specs=pl.BlockSpec(memory_space=pltpu.VMEM),
        scratch_shapes=[
            vmem(block, f32),
            vmem((FIELDS, rows + 8, planes, angles), f32),
            vmem(block, f32),
            vmem(block, f32),
            vmem(pieces, f32),
            vmem(pieces, f32),
            vmem(block, f32),
            vmem((2, blocks, lines, angles), bf16),
            vmem((2, blocks, lines, angles), bf16),
            vmem((2, lines, half), bf16),
            vmem((2, lines, half), bf16),
        ] + [dma((FIELDS, blocks))] * 6 + [dma((3,))] * 2,
        compiler_params=pltpu.CompilerParams(
            collective_id=0, has_side_effects=True, vmem_limit_bytes=63 * 2**20
        ),
    )(density, momentum, energy, trig, filt, jnp.asarray(high), jnp.asarray(low))
    conserved = jnp.concatenate([density[None], momentum, energy[None]], axis=0)
    register_new = SECTION_DECAY * register - COURANT * spacing * term
    state_new = conserved + SECTION_GAIN * register_new
    return (register_new, state_new)


def solution(mesh):
    placed = (
        P("rad", "ax", "azi"),
        P(None, "rad", "ax", "azi"),
        P("rad", "ax", "azi"),
        P(None, "rad", "ax", "azi"),
    )
    return jax.shard_map(
        per_device,
        mesh=mesh,
        in_specs=placed,
        out_specs=(P(None, "rad", "ax", "azi"), P(None, "rad", "ax", "azi")),
        check_vma=False,
    )
```
